512 devices in a mesh: dp: 2 (over z_hi), row: 8 (over z_lo, core), col: 32 (over x, y).
Axes of the slice: x: 4, y: 8, z: 8 (z_hi: 2, z_lo: 4; z = z_hi * 4 + z_lo), core: 2. Of those that a mesh axis runs over, the one named last changes fastest.
Arguments:
- grads: bfloat16 [2, 4, 6144, 6144], P('dp', None, 'col', 'row'), as said below
- params: float32 [4, 6144, 6144], P('dp', 'col', 'row'), may hold values from -6 to 6
- row_moments: float32 [4, 6144], P('dp', 'row'), may hold values from 0.2 to 5
- col_moments: float32 [4, 6144], P('dp', 'col'), may hold values from 0.2 to 5
Outputs:
- new_params: float32 [4, 6144, 6144], P('dp', 'col', 'row')
- update: float32 [4, 6144, 6144], P('dp', 'col', 'row')
- new_row_moments: float32 [4, 6144], P('dp', 'row')
- new_col_moments: float32 [4, 6144], P('dp', 'col')
- row_mean: float32 [4], P('dp')
The draws below stay inside these ranges and needn't reach their ends.
Inputs may be any that keep to these rules, and one draw needn't show every extreme that they name: `grads`: each replica's share of the gradient, finite.
All inputs are finite; a program needn't handle non-finite values.
Results may differ from the reference program's by a relative error of at most 0.0003.
Values sent between devices are 32-bit elements; how exact they have to be, the bound alone decides.
No kernel may reach another device: no remote copies, remote signals or barrier semaphores. Data moves between devices by JAX's collectives and lax.ppermute only.
A program may use at most 64 MiB of HBM per device.

```python
import math
import jax
import jax.numpy as jnp
from jax import lax

D = 6144
LAYERS = 4
REPLICAS = 2


def draw_grads(key, part):
    key = jax.random.fold_in(key, 11)
    key_rows, key_cols, key_noise = jax.random.split(key, 3)
    low, high = (0.3, 3.0)
    ramp = jnp.sqrt(1.0 + 2.0 * jnp.arange(D, dtype=jnp.float32) / (D - 1))
    rows_scale = jnp.exp(jax.random.uniform(key_rows, (LAYERS, 1, D), jnp.float32, math.log(low), math.log(high))) * ramp[None, None, :]
    cols_scale = jnp.exp(jax.random.uniform(key_cols, (LAYERS, D, 1), jnp.float32, math.log(low), math.log(high))) * ramp[None, :, None]
    noise = jax.random.normal(key_noise, (REPLICAS, LAYERS, D, D), jnp.float32)
    return (noise * rows_scale[None] * cols_scale[None]).astype(jnp.bfloat16)


def block_levels(rng, shape, pieces, low, high):
    level = 1.0
    for dim, blocks in pieces:
        heights = jax.random.uniform(jax.random.fold_in(jax.random.fold_in(rng, 6), dim), (blocks,), jnp.float32, low / len(pieces), high / len(pieces))
        level = level * jnp.repeat(jnp.exp(heights), shape[dim] // blocks).reshape((-1,) + (1,) * (len(shape) - 1 - dim))
    return level


def gaussian(own_key, dims, spread, bound, pieces=(), kind=jnp.bfloat16):
    result = spread * jax.random.normal(own_key, dims, jnp.float32)
    if pieces:
        result = result * block_levels(own_key, dims, pieces, -0.22, 0.18)
    return jnp.clip(result, -bound, bound).astype(kind)


def setup_inputs(seed: int = 0) -> dict:
    arg_keys = jax.random.split(jax.random.key(seed), 5)
    grads = draw_grads(jax.random.fold_in(arg_keys[4], 71), 0)
    params = gaussian(arg_keys[1], (LAYERS, D, D), 1.0, 6.0, ((0, 2), (1, 32), (2, 8)), jnp.float32)
    row_moments = jnp.clip(jnp.exp(math.log(5.0) - 3.218876 * jax.random.uniform(arg_keys[2], (LAYERS, D), jnp.float32) ** block_levels(arg_keys[2], (LAYERS, D), ((0, 2), (1, 8)), -0.2, 0.2)), 0.2, 5.0)
    col_moments = jnp.clip(jnp.exp(math.log(5.0) - 3.218876 * jax.random.uniform(arg_keys[3], (LAYERS, D), jnp.float32) ** block_levels(arg_keys[3], (LAYERS, D), ((0, 2), (1, 32)), -0.2, 0.2)), 0.2, 5.0)
    return dict(grads=grads, params=params, row_moments=row_moments, col_moments=col_moments)


def one_matrix(inputs):
    shares, weights, rows_old, cols_old = inputs
    grad = lax.optimization_barrier(jnp.sum(shares.astype(jnp.float32), axis=0))
    square = grad * grad + 1e-30
    new_rows = 0.8 * rows_old + 0.2 * lax.optimization_barrier(jnp.mean(square, axis=0))
    new_cols = 0.8 * cols_old + 0.2 * lax.optimization_barrier(jnp.mean(square, axis=1))
    row_mean = jnp.mean(new_rows)
    raw = grad * lax.rsqrt(new_cols[:, None] * new_rows[None, :] / row_mean)
    clip = jnp.maximum(jnp.float32(1.0), jnp.sqrt(jnp.mean(raw * raw)))
    update = raw / clip
    return (weights - 0.01 * update, update, new_rows, new_cols, row_mean)

def reference(grads, params, row_moments, col_moments):
    stacked = jnp.moveaxis(grads, 1, 0)
    new_params, update, new_rows, new_cols, row_mean = lax.map(one_matrix, (stacked, params, row_moments, col_moments))
    return (new_params, update, new_rows, new_cols, row_mean)
```

```python
import jax
import jax.numpy as jnp
from jax import lax
from jax.sharding import PartitionSpec as P

D = 6144


def gather_sum(x, axis, size):
    copies = jnp.broadcast_to(x[None], (size,) + x.shape)
    return jnp.sum(lax.all_to_all(copies, axis, 0, 0, tiled=True), axis=0)


def per_device(n_row, n_col, grads, params, row_moments, col_moments):
    shares = grads[0]
    half = shares.shape[0] // 2
    me = lax.axis_index("dp")
    give = lax.dynamic_slice_in_dim(shares, (1 - me) * half, half, 0).astype(jnp.float32)
    got = lax.ppermute(give, "dp", [(0, 1), (1, 0)])
    keep = lax.dynamic_slice_in_dim(shares, me * half, half, 0).astype(jnp.float32)
    grad = keep + got

    width = jnp.float32(D)
    square = grad * grad + 1e-30
    row_part = jnp.sum(square, axis=1)
    col_part = jnp.sum(square, axis=2)
    new_cols = 0.8 * col_moments + 0.2 * (gather_sum(col_part, "row", n_row) / width)
    weighed = jnp.sum(grad * grad * (1.0 / new_cols)[:, :, None], axis=1)
    both = gather_sum(jnp.concatenate([row_part, weighed], axis=0), "col", n_col)
    new_rows = 0.8 * row_moments + 0.2 * (both[:half] / width)
    tail = jnp.concatenate([jnp.sum(new_rows, axis=1), jnp.sum(both[half:] / new_rows, axis=1)])
    total = gather_sum(tail, "row", n_row)
    row_mean = total[:half] / width
    squares_sum = row_mean * total[half:]
    clip = jnp.maximum(jnp.float32(1.0), jnp.sqrt(squares_sum / (width * width)))
    scale = lax.rsqrt(new_cols) * (jnp.sqrt(row_mean) / clip)[:, None]
    update = grad * lax.rsqrt(new_rows)[:, None, :] * scale[:, :, None]
    return (params - 0.01 * update, update, new_rows, new_cols, row_mean)


def solution(mesh):
    n_row, n_col = mesh.shape["row"], mesh.shape["col"]
    return jax.shard_map(
        lambda *args: per_device(n_row, n_col, *args),
        mesh=mesh,
        in_specs=(
            P("dp", None, "col", "row"),
            P("dp", "col", "row"),
            P("dp", "row"),
            P("dp", "col"),
        ),
        out_specs=(
            P("dp", "col", "row"),
            P("dp", "col", "row"),
            P("dp", "row"),
            P("dp", "col"),
            P("dp"),
        ),
        check_vma=False,
    )
```

```python
import jax
import jax.numpy as jnp
from jax import lax
from jax.sharding import PartitionSpec as P

D = 6144


def gather_sum(x, axis, size):
    copies = jnp.broadcast_to(x[None], (size,) + x.shape)
    return jnp.sum(lax.all_to_all(copies, axis, 0, 0, tiled=True), axis=0)


def per_device(n_row, n_col, grads, params, row_moments, col_moments):
    shares = grads[0]
    half = shares.shape[0] // 2
    me = lax.axis_index("dp")
    width = jnp.float32(D)

    def layer(first, k):
        return lax.dynamic_index_in_dim(shares, first * half + k, 0, keepdims=False).astype(jnp.float32)

    got, after = [], shares
    for k in range(half):
        got.append(lax.ppermute(layer(1 - me, k), "dp", [(0, 1), (1, 0)]))

    grad, new_rows, new_cols, tails = [], [], [], []
    for k in range(half):
        if k:
            got[k], new_rows[k - 1], tails[k - 1] = lax.optimization_barrier((got[k], new_rows[k - 1], tails[k - 1]))
        g = layer(me, k) + got[k]
        square = g * g + 1e-30
        row_part = jnp.sum(square, axis=0)
        col_part = jnp.sum(square, axis=1)
        cols = 0.8 * col_moments[k] + 0.2 * (gather_sum(col_part, "row", n_row) / width)
        weighed = jnp.sum(g * g * (1.0 / cols)[:, None], axis=0)
        both = gather_sum(jnp.stack([row_part, weighed]), "col", n_col)
        rows = 0.8 * row_moments[k] + 0.2 * (both[0] / width)
        grad.append(g)
        new_rows.append(rows)
        new_cols.append(cols)
        tails.append(jnp.stack([jnp.sum(rows), jnp.sum(both[1] / rows)]))

    total = gather_sum(jnp.stack(tails), "row", n_row)
    row_mean = total[:, 0] / width
    squares_sum = row_mean * total[:, 1]
    clip = jnp.maximum(jnp.float32(1.0), jnp.sqrt(squares_sum / (width * width)))
    scale = jnp.sqrt(row_mean) / clip
    update = jnp.stack(
        [
            grad[k] * lax.rsqrt(new_rows[k])[None, :] * (lax.rsqrt(new_cols[k]) * scale[k])[:, None]
            for k in range(half)
        ]
    )
    return (params - 0.01 * update, update, jnp.stack(new_rows), jnp.stack(new_cols), row_mean)


def solution(mesh):
    n_row, n_col = mesh.shape["row"], mesh.shape["col"]
    return jax.shard_map(
        lambda *args: per_device(n_row, n_col, *args),
        mesh=mesh,
        in_specs=(
            P("dp", None, "col", "row"),
            P("dp", "col", "row"),
            P("dp", "row"),
            P("dp", "col"),
        ),
        out_specs=(
            P("dp", "col", "row"),
            P("dp", "col", "row"),
            P("dp", "row"),
            P("dp", "col"),
            P("dp"),
        ),
        check_vma=False,
    )
```

```python
import jax
import jax.numpy as jnp
from jax import lax
from jax.sharding import PartitionSpec as P

D = 6144


def gather_sum(x, axis, size):
    copies = jnp.broadcast_to(x[None], (size,) + x.shape)
    return jnp.sum(lax.all_to_all(copies, axis, 0, 0, tiled=True), axis=0)


def per_device(n_row, n_col, grads, params, row_moments, col_moments):
    shares = grads[0]
    me = lax.axis_index("dp")
    width = jnp.float32(D)
    rows = row_moments.shape[1]

    def layer(first, k):
        return lax.dynamic_slice_in_dim(shares, first * 2 + k, 1, 0).astype(jnp.float32)

    def mean_in(old, total):
        return 0.8 * old + 0.2 * (total / width)

    got = [lax.ppermute(layer(1 - me, k), "dp", [(0, 1), (1, 0)]) for k in range(2)]

    def early(got0, rows_old):
        g = lax.optimization_barrier(layer(me, 0) + got0)
        square = g * g + 1e-30
        row_sum = gather_sum(jnp.sum(square, axis=1), "col", n_col)
        weighed = jnp.sum(g * g * (1.0 / mean_in(rows_old, row_sum))[:, None, :], axis=2)
        return g, row_sum, jnp.concatenate([jnp.sum(square, axis=2), weighed])

    def never(got0, rows_old):
        return got0, rows_old, got0[:, :, :2].reshape(2, -1)

    g0, row_sum0, cols0 = lax.cond(me < 2, early, never, got[0], row_moments[:1])
    got1, row_sum0, cols0 = lax.optimization_barrier((got[1], row_sum0, cols0))

    g1 = lax.optimization_barrier(layer(me, 1) + got1)
    square = g1 * g1 + 1e-30
    row_part = jnp.sum(square, axis=1)
    sums = gather_sum(jnp.concatenate([cols0[:1], jnp.sum(square, axis=2), cols0[1:], cols0[1:]], axis=0), "row", n_row)
    new_cols = mean_in(col_moments, sums[:2])
    weighed = jnp.sum(g1 * g1 * (1.0 / new_cols[1:])[:, :, None], axis=1)
    packed = jnp.concatenate([row_part, weighed, sums[2:3] / new_cols[:1]], axis=1)
    both = gather_sum(packed, "col", n_col)
    new_rows = mean_in(row_moments, jnp.concatenate([row_sum0, both[:, :rows]]))
    whole = jnp.pad(both[:, 2 * rows :] * (1.0 / n_row), ((0, 0), (0, 3 * rows - both.shape[1])))
    raw = jnp.concatenate([whole, both[:, rows : 2 * rows] / new_rows[1:]])
    tail = jnp.concatenate([jnp.sum(new_rows, axis=1), jnp.sum(raw, axis=1)])
    total = gather_sum(tail, "row", n_row)
    row_mean = total[:2] / width
    squares_sum = row_mean * total[2:]
    clip = jnp.maximum(jnp.float32(1.0), jnp.sqrt(squares_sum / (width * width)))
    scale = lax.rsqrt(new_cols) * (jnp.sqrt(row_mean) / clip)[:, None]
    grad = jnp.concatenate([g0, g1])
    update = grad * lax.rsqrt(new_rows)[:, None, :] * scale[:, :, None]
    return (params - 0.01 * update, update, new_rows, new_cols, row_mean)


def solution(mesh):
    n_row, n_col = mesh.shape["row"], mesh.shape["col"]
    return jax.shard_map(
        lambda *args: per_device(n_row, n_col, *args),
        mesh=mesh,
        in_specs=(
            P("dp", None, "col", "row"),
            P("dp", "col", "row"),
            P("dp", "row"),
            P("dp", "col"),
        ),
        out_specs=(
            P("dp", "col", "row"),
            P("dp", "col", "row"),
            P("dp", "row"),
            P("dp", "col"),
            P("dp"),
        ),
        check_vma=False,
    )
```

```python
import jax
import jax.numpy as jnp
from jax import lax
from jax.experimental import pallas as pl
from jax.experimental.pallas import tpu as pltpu
from jax.sharding import PartitionSpec as P

D = 6144
PIECES = 2


def gather_sum(x, axis, size):
    copies = jnp.broadcast_to(x[None], (size,) + x.shape)
    return jnp.sum(lax.all_to_all(copies, axis, 0, 0, tiled=True), axis=0)


def finish_kernel(
    tails_ref, g0_ref, g1_ref, params_ref, rows_ref, cols_ref,
    new_params_ref, update_ref, row_mean_out, params_out, update_out, means, sems, mean_sem,
):
    width = jnp.float32(D)
    total = jnp.sum(tails_ref[...], axis=0)
    columns, rows = g0_ref.shape[1:]
    step = columns // PIECES
    for k in range(2):
        means[k] = (total[:, k : k + 1] / width)[0, 0]
    copies = [pltpu.make_async_copy(means, row_mean_out, mean_sem)]
    copies[0].start()
    for k, g_ref in enumerate((g0_ref, g1_ref)):
        row_mean = total[:, k : k + 1] / width
        squares_sum = row_mean * total[:, k + 2 : k + 3]
        clip = jnp.maximum(jnp.float32(1.0), jnp.sqrt(squares_sum / (width * width)))
        scale = lax.rsqrt(cols_ref[k : k + 1, :]) * (jnp.sqrt(row_mean) / clip)
        scale = jnp.broadcast_to(scale, (128, columns)).T
        per_row = lax.rsqrt(rows_ref[k : k + 1, :])
        for p in range(PIECES):
            part = pl.ds(p * step, step)
            for q in range(rows // 128):
                lanes = pl.ds(q * 128, 128)
                update = (
                    g_ref[0, part, lanes]
                    * per_row[:, q * 128 : (q + 1) * 128]
                    * scale[p * step : (p + 1) * step, :]
                )
                update_out[k, part, lanes] = update
                params_out[k, part, lanes] = params_ref[k, part, lanes] - 0.01 * update
            for n, (source, target) in enumerate(((update_out, update_ref), (params_out, new_params_ref))):
                copy = pltpu.make_async_copy(source.at[k, part], target.at[k, part], sems.at[n, k * PIECES + p])
                copy.start()
                copies.append(copy)
    for copy in copies:
        copy.wait()


def finish(tails, g0, g1, params, new_rows, new_cols):
    whole = jax.ShapeDtypeStruct(params.shape, jnp.float32)
    vmem = pl.BlockSpec(memory_space=pltpu.VMEM)
    return pl.pallas_call(
        finish_kernel,
        out_shape=(whole, whole, jax.ShapeDtypeStruct((2,), jnp.float32)),
        in_specs=[vmem] * 6,
        out_specs=(
            pl.BlockSpec(memory_space=pl.ANY),
            pl.BlockSpec(memory_space=pl.ANY),
            pl.BlockSpec(memory_space=pl.ANY),
        ),
        scratch_shapes=[
            pltpu.VMEM(params.shape, jnp.float32),
            pltpu.VMEM(params.shape, jnp.float32),
            pltpu.SMEM((2,), jnp.float32),
            pltpu.SemaphoreType.DMA((2, 2 * PIECES)),
            pltpu.SemaphoreType.DMA,
        ],
        compiler_params=pltpu.CompilerParams(vmem_limit_bytes=16 << 20),
    )(tails, g0, g1, params, new_rows, new_cols)

def per_device(n_row, n_col, grads, params, row_moments, col_moments):
    shares = grads[0]
    me = lax.axis_index("dp")
    width = jnp.float32(D)
    rows = row_moments.shape[1]

    def layer(first, k):
        return lax.dynamic_slice_in_dim(shares, first * 2 + k, 1, 0).astype(jnp.float32)

    def mean_in(old, total):
        return 0.8 * old + 0.2 * (total / width)

    got = [lax.ppermute(layer(1 - me, k), "dp", [(0, 1), (1, 0)]) for k in range(2)]

    def early(got0, rows_old):
        g = lax.optimization_barrier(layer(me, 0) + got0)
        square = g * g + 1e-30
        row_sum = gather_sum(jnp.sum(square, axis=1), "col", n_col)
        weighed = jnp.sum(g * g * (1.0 / mean_in(rows_old, row_sum))[:, None, :], axis=2)
        return g, row_sum, jnp.concatenate([jnp.sum(square, axis=2), weighed])

    def never(got0, rows_old):
        return got0, rows_old, got0[:, :, :2].reshape(2, -1)

    g0, row_sum0, cols0 = lax.cond(me < 2, early, never, got[0], row_moments[:1])
    got1, row_sum0, cols0 = lax.optimization_barrier((got[1], row_sum0, cols0))

    g1 = lax.optimization_barrier(layer(me, 1) + got1)
    square = g1 * g1 + 1e-30
    row_part = jnp.sum(square, axis=1)
    sums = gather_sum(jnp.concatenate([cols0[:1], jnp.sum(square, axis=2), cols0[1:], cols0[1:]], axis=0), "row", n_row)
    new_cols = mean_in(col_moments, sums[:2])
    weighed = jnp.sum(g1 * g1 * (1.0 / new_cols[1:])[:, :, None], axis=1)
    packed = jnp.concatenate([row_part, weighed, sums[2:3] / new_cols[:1]], axis=1)
    both = gather_sum(packed, "col", n_col)
    new_rows = mean_in(row_moments, jnp.concatenate([row_sum0, both[:, :rows]]))
    whole = jnp.pad(both[:, 2 * rows :] * (1.0 / n_row), ((0, 0), (0, 3 * rows - both.shape[1])))
    raw = jnp.concatenate([whole, both[:, rows : 2 * rows] / new_rows[1:]])
    tail = jnp.concatenate([jnp.sum(new_rows, axis=1), jnp.sum(raw, axis=1)])
    copies = jnp.broadcast_to(tail, (n_row, 1, 4))
    tails = lax.all_to_all(copies, "row", 0, 0, tiled=True)
    new_params, update, row_mean = finish(tails, g0, g1, params, new_rows, new_cols)
    return (new_params, update, new_rows, new_cols, row_mean)


def solution(mesh):
    n_row, n_col = mesh.shape["row"], mesh.shape["col"]
    return jax.shard_map(
        lambda *args: per_device(n_row, n_col, *args),
        mesh=mesh,
        in_specs=(
            P("dp", None, "col", "row"),
            P("dp", "col", "row"),
            P("dp", "row"),
            P("dp", "col"),
        ),
        out_specs=(
            P("dp", "col", "row"),
            P("dp", "col", "row"),
            P("dp", "row"),
            P("dp", "col"),
            P("dp"),
        ),
        check_vma=False,
    )
```

```python
import jax
import jax.numpy as jnp
from jax import lax
from jax.experimental import pallas as pl
from jax.experimental.pallas import tpu as pltpu
from jax.sharding import PartitionSpec as P

D = 6144
PIECES = 2


def gather_sum(x, axis, size):
    copies = jnp.broadcast_to(x[None], (size,) + x.shape)
    return jnp.sum(lax.all_to_all(copies, axis, 0, 0, tiled=True), axis=0)


def finish_kernel(
    tails_ref, g0_ref, g1_ref, params_ref, rows_ref, cols_ref,
    new_params_ref, update_ref, row_mean_out, params_out, update_out, means, sems, mean_sem,
):
    width = jnp.float32(D)
    total = jnp.sum(tails_ref[...], axis=0)
    columns, rows = g0_ref.shape[1:]
    step = columns // PIECES
    for k in range(2):
        means[k] = (total[:, k : k + 1] / width)[0, 0]
    copies = [pltpu.make_async_copy(means, row_mean_out, mean_sem)]
    copies[0].start()
    for k, g_ref in enumerate((g0_ref, g1_ref)):
        row_mean = total[:, k : k + 1] / width
        squares_sum = row_mean * total[:, k + 2 : k + 3]
        clip = jnp.maximum(jnp.float32(1.0), jnp.sqrt(squares_sum / (width * width)))
        scale = lax.rsqrt(cols_ref[k : k + 1, :]) * (jnp.sqrt(row_mean) / clip)
        scale = jnp.broadcast_to(scale, (128, columns)).T
        per_row = lax.rsqrt(rows_ref[k : k + 1, :])
        for p in range(PIECES):
            part = pl.ds(p * step, step)
            for q in range(rows // 128):
                lanes = pl.ds(q * 128, 128)
                update = (
                    g_ref[0, part, lanes]
                    * per_row[:, q * 128 : (q + 1) * 128]
                    * scale[p * step : (p + 1) * step, :]
                )
                update_out[k, part, lanes] = update
                params_out[k, part, lanes] = params_ref[k, part, lanes] - 0.01 * update
            for n, (source, target) in enumerate(((update_out, update_ref), (params_out, new_params_ref))):
                copy = pltpu.make_async_copy(source.at[k, part], target.at[k, part], sems.at[n, k * PIECES + p])
                copy.start()
                copies.append(copy)
    for copy in copies:
        copy.wait()


def finish(tails, g0, g1, params, new_rows, new_cols):
    whole = jax.ShapeDtypeStruct(params.shape, jnp.float32)
    vmem = pl.BlockSpec(memory_space=pltpu.VMEM)
    return pl.pallas_call(
        finish_kernel,
        out_shape=(whole, whole, jax.ShapeDtypeStruct((2,), jnp.float32)),
        in_specs=[vmem] * 6,
        out_specs=(
            pl.BlockSpec(memory_space=pl.ANY),
            pl.BlockSpec(memory_space=pl.ANY),
            pl.BlockSpec(memory_space=pl.ANY),
        ),
        scratch_shapes=[
            pltpu.VMEM(params.shape, jnp.float32),
            pltpu.VMEM(params.shape, jnp.float32),
            pltpu.SMEM((2,), jnp.float32),
            pltpu.SemaphoreType.DMA((2, 2 * PIECES)),
            pltpu.SemaphoreType.DMA,
        ],
        compiler_params=pltpu.CompilerParams(vmem_limit_bytes=16 << 20),
    )(tails, g0, g1, params, new_rows, new_cols)

def per_device(n_row, n_col, grads, params, row_moments, col_moments):
    shares = grads[0]
    me = lax.axis_index("dp")
    width = jnp.float32(D)
    rows = row_moments.shape[1]

    def layer(first, k):
        return lax.dynamic_slice_in_dim(shares, first * 2 + k, 1, 0).astype(jnp.float32)

    def mean_in(old, total):
        return 0.8 * old + 0.2 * (total / width)

    got = [lax.ppermute(layer(1 - me, k), "dp", [(0, 1), (1, 0)]) for k in range(2)]

    def early(got0, rows_old):
        g = lax.optimization_barrier(layer(me, 0) + got0)
        square = g * g + 1e-30
        row_sum = gather_sum(jnp.sum(square, axis=1), "col", n_col)
        weighed = jnp.sum(g * g * (1.0 / mean_in(rows_old, row_sum))[:, None, :], axis=2)
        return g, row_sum, jnp.concatenate([jnp.sum(square, axis=2), weighed])

    def never(got0, rows_old):
        return got0, rows_old, got0[:, :, :2].reshape(2, -1)

    g0, row_sum0, cols0 = lax.cond(me < 2, early, never, got[0], row_moments[:1])
    got1, row_sum0, cols0 = lax.optimization_barrier((got[1], row_sum0, cols0))

    g1 = lax.optimization_barrier(layer(me, 1) + got1)
    square = g1 * g1 + 1e-30
    row_part = jnp.sum(square, axis=1)
    sums = gather_sum(jnp.concatenate([cols0[:1], jnp.sum(square, axis=2), cols0[1:], cols0[1:]], axis=0), "row", n_row)
    new_cols = mean_in(col_moments, sums[:2])
    weighed = jnp.sum(g1 * g1 * (1.0 / new_cols[1:])[:, :, None], axis=1)
    share = sums[2:3] / new_cols[:1]
    cut = share.shape[1] // 2
    packed = jnp.concatenate(
        [
            jnp.concatenate([row_part, share[:, :cut]], axis=1),
            jnp.concatenate([weighed, share[:, cut:]], axis=1),
        ]
    )
    both = gather_sum(packed, "col", n_col)
    new_rows = mean_in(row_moments, jnp.concatenate([row_sum0, both[:1, :rows]]))
    whole = (both[:1, rows:] + both[1:, rows:]) * (1.0 / n_row)
    whole = jnp.pad(whole, ((0, 0), (0, rows - whole.shape[1])))
    raw = jnp.concatenate([whole, both[1:, :rows] / new_rows[1:]])
    tail = jnp.concatenate([jnp.sum(new_rows, axis=1), jnp.sum(raw, axis=1)])
    copies = jnp.broadcast_to(tail, (n_row, 1, 4))
    tails = lax.all_to_all(copies, "row", 0, 0, tiled=True)
    new_params, update, row_mean = finish(tails, g0, g1, params, new_rows, new_cols)
    return (new_params, update, new_rows, new_cols, row_mean)


def solution(mesh):
    n_row, n_col = mesh.shape["row"], mesh.shape["col"]
    return jax.shard_map(
        lambda *args: per_device(n_row, n_col, *args),
        mesh=mesh,
        in_specs=(
            P("dp", None, "col", "row"),
            P("dp", "col", "row"),
            P("dp", "row"),
            P("dp", "col"),
        ),
        out_specs=(
            P("dp", "col", "row"),
            P("dp", "col", "row"),
            P("dp", "row"),
            P("dp", "col"),
            P("dp"),
        ),
        check_vma=False,
    )
```

```python
import jax
import jax.numpy as jnp
from jax import lax
from jax.experimental import pallas as pl
from jax.experimental.pallas import tpu as pltpu
from jax.sharding import PartitionSpec as P

D = 6144
PIECES = 2


def gather_sum(x, axis, size):
    copies = jnp.broadcast_to(x[None], (size,) + x.shape)
    return jnp.sum(lax.all_to_all(copies, axis, 0, 0, tiled=True), axis=0)


def finish_kernel(
    tails_ref, g0_ref, g1_ref, params_ref, rows_ref, cols_ref,
    new_params_ref, update_ref, row_mean_out, params_out, update_out, means, sems, mean_sem,
):
    width = jnp.float32(D)
    total = jnp.sum(tails_ref[...], axis=0)
    columns, rows = g0_ref.shape[1:]
    step = columns // PIECES
    for k in range(2):
        means[k] = (total[:, k : k + 1] / width)[0, 0]
    copies = [pltpu.make_async_copy(means, row_mean_out, mean_sem)]
    copies[0].start()
    for k, g_ref in enumerate((g0_ref, g1_ref)):
        row_mean = total[:, k : k + 1] / width
        squares_sum = row_mean * total[:, k + 2 : k + 3]
        clip = jnp.maximum(jnp.float32(1.0), jnp.sqrt(squares_sum / (width * width)))
        scale = lax.rsqrt(cols_ref[k : k + 1, :]) * (jnp.sqrt(row_mean) / clip)
        scale = jnp.broadcast_to(scale, (128, columns)).T
        per_row = lax.rsqrt(rows_ref[k : k + 1, :])
        for p in range(PIECES):
            part = pl.ds(p * step, step)
            for q in range(rows // 128):
                lanes = pl.ds(q * 128, 128)
                update = (
                    g_ref[0, part, lanes]
                    * per_row[:, q * 128 : (q + 1) * 128]
                    * scale[p * step : (p + 1) * step, :]
                )
                update_out[k, part, lanes] = update
                params_out[k, part, lanes] = params_ref[k, part, lanes] - 0.01 * update
            for n, (source, target) in enumerate(((update_out, update_ref), (params_out, new_params_ref))):
                copy = pltpu.make_async_copy(source.at[k, part], target.at[k, part], sems.at[n, k * PIECES + p])
                copy.start()
                copies.append(copy)
    for copy in copies:
        copy.wait()


def finish(tails, g0, g1, params, new_rows, new_cols):
    whole = jax.ShapeDtypeStruct(params.shape, jnp.float32)
    vmem = pl.BlockSpec(memory_space=pltpu.VMEM)
    return pl.pallas_call(
        finish_kernel,
        out_shape=(whole, whole, jax.ShapeDtypeStruct((2,), jnp.float32)),
        in_specs=[vmem] * 6,
        out_specs=(
            pl.BlockSpec(memory_space=pl.ANY),
            pl.BlockSpec(memory_space=pl.ANY),
            pl.BlockSpec(memory_space=pl.ANY),
        ),
        scratch_shapes=[
            pltpu.VMEM(params.shape, jnp.float32),
            pltpu.VMEM(params.shape, jnp.float32),
            pltpu.SMEM((2,), jnp.float32),
            pltpu.SemaphoreType.DMA((2, 2 * PIECES)),
            pltpu.SemaphoreType.DMA,
        ],
        compiler_params=pltpu.CompilerParams(vmem_limit_bytes=16 << 20),
    )(tails, g0, g1, params, new_rows, new_cols)

def per_device(n_row, n_col, grads, params, row_moments, col_moments):
    shares = grads[0]
    me = lax.axis_index("dp")
    width = jnp.float32(D)
    rows = row_moments.shape[1]

    def layer(first, k):
        return lax.dynamic_slice_in_dim(shares, first * 2 + k, 1, 0).astype(jnp.float32)

    def mean_in(old, total):
        return 0.8 * old + 0.2 * (total / width)

    got = [lax.ppermute(layer(1 - me, k), "dp", [(0, 1), (1, 0)]) for k in range(2)]

    def early(got0, rows_old):
        g = lax.optimization_barrier(layer(me, 0) + got0)
        square = g * g + 1e-30
        row_sum = gather_sum(jnp.sum(square, axis=1), "col", n_col)
        weighed = jnp.sum(g * g * (1.0 / mean_in(rows_old, row_sum))[:, None, :], axis=2)
        return g, row_sum, jnp.concatenate([jnp.sum(square, axis=2), weighed])

    def never(got0, rows_old):
        return got0, rows_old, got0[:, :, :2].reshape(2, -1)

    g0, row_sum0, cols0 = lax.cond(me < 2, early, never, got[0], row_moments[:1])
    got1, row_sum0, cols0 = lax.optimization_barrier((got[1], row_sum0, cols0))

    g1 = lax.optimization_barrier(layer(me, 1) + got1)
    square = g1 * g1 + 1e-30
    row_part = jnp.sum(square, axis=1)
    sums = gather_sum(jnp.concatenate([cols0[:1], jnp.sum(square, axis=2), cols0[1:]], axis=0), "row", n_row)
    new_cols = mean_in(col_moments, sums[:2])
    weighed = jnp.sum(g1 * g1 * (1.0 / new_cols[1:])[:, :, None], axis=1)
    packed = jnp.concatenate([row_part, weighed, sums[2:3] / new_cols[:1]], axis=1)
    both = gather_sum(packed, "col", n_col)
    new_rows = mean_in(row_moments, jnp.concatenate([row_sum0, both[:, :rows]]))
    whole = jnp.pad(both[:, 2 * rows :] * (1.0 / n_row), ((0, 0), (0, 3 * rows - both.shape[1])))
    raw = jnp.concatenate([whole, both[:, rows : 2 * rows] / new_rows[1:]])
    tail = jnp.concatenate([jnp.sum(new_rows, axis=1), jnp.sum(raw, axis=1)])
    copies = jnp.broadcast_to(tail, (n_row, 1, 4))
    tails = lax.all_to_all(copies, "row", 0, 0, tiled=True)
    new_params, update, row_mean = finish(tails, g0, g1, params, new_rows, new_cols)
    return (new_params, update, new_rows, new_cols, row_mean)


def solution(mesh):
    n_row, n_col = mesh.shape["row"], mesh.shape["col"]
    return jax.shard_map(
        lambda *args: per_device(n_row, n_col, *args),
        mesh=mesh,
        in_specs=(
            P("dp", None, "col", "row"),
            P("dp", "col", "row"),
            P("dp", "row"),
            P("dp", "col"),
        ),
        out_specs=(
            P("dp", "col", "row"),
            P("dp", "col", "row"),
            P("dp", "row"),
            P("dp", "col"),
            P("dp"),
        ),
        check_vma=False,
    )
```
